128 devices in a mesh: group: 4 (over y), local: 32 (over z, x, core).
Axes of the slice: x: 4, y: 4, z: 4, core: 2. Of those that a mesh axis runs over, the one named last changes fastest.
Arguments:
- tokens: bfloat16 [8192, 7168], P(('group', 'local')), may hold values from -6 to 6
- routes: int32 [8192, 8], P(('group', 'local')), may hold values from 0 to 63, all different within a row; in each aligned block of 64 rows (0 to 63, 64 to 127, ...) at most 10 rows name the same one
- gates: float32 [8192, 8], P(('group', 'local')), may hold values from 0.05 to 1
- gate_weight: bfloat16 [128, 7168, 512], P(('group', 'local')), may hold values from -0.0625 to 0.0625
- up_weight: bfloat16 [128, 7168, 512], P(('group', 'local')), may hold values from -0.0625 to 0.0625
- down_weight: bfloat16 [128, 512, 7168], P(('group', 'local')), may hold values from -0.1875 to 0.1875
Outputs:
- mixed: bfloat16 [8192, 7168], P(('group', 'local'))
The draws below stay inside these ranges and needn't reach their ends.
Inputs may be any that keep to these rules, and one draw needn't show every extreme that they name: `routes`: each row names 8 different experts. Among the 64 rows of one device no expert is named by more than 10 rows, a bound that some block reaches.
All inputs are finite; a program needn't handle non-finite values.
Results may differ from the reference program's by a relative error of at most 0.0065.
Values may be sent and summed in bfloat16 or wider, within the bound.
No kernel may reach another device: no remote copies, remote signals or barrier semaphores. Data moves between devices by JAX's collectives and lax.ppermute only.
A program may use at most 192 MiB of HBM per device.

```python
import math
import jax
import jax.numpy as jnp
import numpy as np
from jax import lax

D = 7168
FF = 1024
TOPK = 8
TOK_DEV = 64
FF_DEV = 512
EXPERTS = 64
CAP = 10
TOKENS = 8192
N_GROUP = 4
N_LOCAL = 32


def level_of(own_key, dims, shards, low, largest):
    factor_of = 1.0
    for axis_at, shards_of in shards:
        heights = jax.random.uniform(jax.random.fold_in(jax.random.fold_in(own_key, 6), axis_at), (shards_of,), jnp.float32, low / len(shards), largest / len(shards))
        factor_of = factor_of * jnp.repeat(jnp.exp(heights), dims[axis_at] // shards_of).reshape((-1,) + (1,) * (len(dims) - 1 - axis_at))
    return factor_of


def shared_out(stream_key, own, number, rows, count, top, limit, lean):
    sequence = jax.random.permutation(stream_key, count)
    packed, usual = shares(count, rows * top, limit, lean, True), shares(count, rows * top, limit, lean, False)
    places = jnp.arange(count)

    def named(sizes, turn):
        used = int((sizes > 0).sum())
        fixed = max(1, used // 4)
        passed = fixed + (places - fixed + turn * (used - fixed)) % max(1, count - fixed)
        return jnp.zeros((count,), jnp.int32).at[sequence[jnp.where(places < fixed, places, passed)]].set(jnp.asarray(sizes, jnp.int32))

    sizes = jnp.where(number % 4 == 0, named(packed, number // 4), named(usual, number - number // 4 - 1))
    mixed = jax.random.permutation(jax.random.fold_in(own, 3), count)
    giver, taker = mixed[0:count // 2 * 2:2], mixed[1:count // 2 * 2:2]
    slack = jnp.minimum(sizes[giver] - 1, limit - sizes[taker]) // 2
    slack = jnp.where((giver == sequence[0]) | (taker == sequence[0]) | (sizes[taker] == 0), 0, jnp.maximum(slack, 0))
    passed = jax.random.randint(jax.random.fold_in(own, 4), (count // 2,), 0, 1 << 20) % (slack + 1)
    sizes = sizes.at[giver].add(-passed).at[taker].add(passed)
    members = jnp.searchsorted(jnp.cumsum(sizes), jnp.arange(rows * top), side="right").astype(jnp.int32)
    grid = members.reshape(top, rows).T
    grid = grid[jax.random.permutation(jax.random.fold_in(own, 1), rows)]
    turn = jax.random.randint(jax.random.fold_in(own, 2), (rows, 1), 0, top)
    return jnp.take_along_axis(grid, (jnp.arange(top)[None, :] + turn) % top, axis=1)


def shares(count, total, limit, skew, full):
    loads = [(1 << 20) // math.isqrt(standing ** skew) + 1 for standing in range(1, count + 1)]
    largest = limit if full else min(limit, max(-(-total // count), total * loads[0] // sum(loads)))
    least = 1 if total - largest >= count - 1 else 0
    counts, rest = [largest] + [least] * (count - 1), total - largest - least * (count - 1)
    while rest > 0:
        movable = [i for i in range(1, count) if counts[i] < largest] or [i for i in range(1, count) if counts[i] < limit]
        mass, remaining = sum([loads[i] for i in movable]), rest
        for i in movable:
            more = min(limit - counts[i], max(1, remaining * loads[i] // mass), rest)
            counts[i] = counts[i] + more
            rest = rest - more
    return np.array(counts)


def noise(stream_key, extent, deviation, limit, pieces=(), kind=jnp.bfloat16):
    drawn = jax.random.normal(stream_key, extent, jnp.float32) * deviation
    if len(pieces) > 0:
        drawn = level_of(stream_key, extent, pieces, -0.22, 0.18) * drawn
    return jnp.clip(drawn, min=-limit, max=limit).astype(kind)


def setup_inputs(seed: int = 0) -> dict:
    key_list = jax.random.split(jax.random.key(seed), 7)
    tokens = noise(key_list[0], (TOKENS, D), 1.0, 6.0, ((0, 128),))
    routes_keys = jax.random.split(jax.random.fold_in(key_list[1], 1), TOKENS // TOK_DEV)
    routes_turns = jax.random.permutation(jax.random.fold_in(key_list[1], 3), TOKENS // TOK_DEV)
    routes = jax.vmap(lambda own, number: shared_out(jax.random.fold_in(key_list[1], 2), own, number, TOK_DEV, EXPERTS, TOPK, CAP, 2))(routes_keys, routes_turns).reshape((TOKENS, TOPK))
    gates = jnp.clip(jnp.exp(math.log(1.0) - 2.9957323 * jax.random.uniform(key_list[2], (TOKENS, TOPK), jnp.float32) ** level_of(key_list[2], (TOKENS, TOPK), ((0, 128),), -0.2, 0.2)), 0.05, 1.0)
    gate_weight = noise(key_list[3], (2 * EXPERTS, D, FF_DEV), D ** -0.5, 0.0625, ((0, 128),))
    up_weight = noise(key_list[4], (2 * EXPERTS, D, FF_DEV), D ** -0.5, 0.0625, ((0, 128),))
    down_weight = noise(key_list[5], (2 * EXPERTS, FF_DEV, D), FF ** -0.5, 0.1875, ((0, 128),))
    return {"tokens": tokens, "routes": routes, "gates": gates, "gate_weight": gate_weight, "up_weight": up_weight, "down_weight": down_weight}


def reference(tokens, routes, gates, gate_weight, up_weight, down_weight):
    experts = gate_weight.shape[0] // 2
    slots_all = N_GROUP * N_LOCAL * CAP
    flat_routes = routes.reshape(-1).astype(jnp.int32)
    count_rows = flat_routes.shape[0]
    hits = (flat_routes[:, None] == jnp.arange(experts, dtype=jnp.int32)[None, :]).astype(jnp.int32)
    earlier = jnp.cumsum(hits, axis=0) - hits
    ranking = jnp.sum(earlier * hits, axis=1).astype(jnp.int32)
    owners = (jnp.arange(count_rows, dtype=jnp.int32) // TOPK).astype(jnp.int32)
    places = (flat_routes * slots_all + ranking).astype(jnp.int32)
    table = jnp.full((experts * slots_all,), TOKENS, dtype=jnp.int32).at[places].set(owners)
    table = table.reshape(experts, slots_all)
    padded = jnp.concatenate([tokens, jnp.zeros((1, tokens.shape[1]), tokens.dtype)], axis=0)

    def half_part(rows_in, row_index):
        gate_val = jnp.dot(rows_in, gate_weight[row_index], preferred_element_type=jnp.float32)
        up_val = jnp.dot(rows_in, up_weight[row_index], preferred_element_type=jnp.float32)
        hidden = (jax.nn.silu(gate_val) * up_val).astype(jnp.bfloat16)
        part = jnp.dot(hidden, down_weight[row_index], preferred_element_type=jnp.float32).astype(jnp.bfloat16)
        return lax.optimization_barrier(part).astype(jnp.float32)

    def one_expert(index):
        rows_in = padded[table[index]]
        first = half_part(rows_in, 2 * index)
        second = half_part(rows_in, 2 * index + 1)
        return (first + second).astype(jnp.bfloat16)

    outputs = lax.map(one_expert, jnp.arange(experts, dtype=jnp.int32))
    picked = outputs.reshape(-1, tokens.shape[1])[places].reshape(routes.shape[0], TOPK, tokens.shape[1])
    mixed = jnp.sum(picked.astype(jnp.float32) * gates[:, :, None], axis=1)
    return mixed.astype(jnp.bfloat16)
```

```python
import functools

import jax
import jax.numpy as jnp
from jax import lax
from jax.experimental import pallas as pl
from jax.experimental.pallas import tpu as pltpu
from jax.sharding import PartitionSpec as P

AXES = ("group", "local")
PARTS = 8
TILE = 32 * PARTS
SLOTS = (5,)
F32 = jnp.float32
BF16 = jnp.bfloat16


def quotient(value, by, most):
    shift = 0
    while True:
        factor = (1 << shift) // by + 1
        if factor * most < 1 << 31 and all(v * factor >> shift == v // by for v in range(most + 1)):
            return lax.shift_right_logical(value * factor, shift)
        shift += 1


def iota(shape, dim):
    return lax.broadcasted_iota(jnp.int32, shape, dim)


def expert_and_rank(row, slots, first, half, most):
    device = quotient(row, slots, most)
    slot = row - device * slots
    return lax.shift_right_logical(device, 1), (device & 1) * half + first + slot


def to_parts(dtype=BF16):
    p, q = iota((TILE, TILE), 0), iota((TILE, TILE), 1)
    return ((p & 31) * PARTS + (p >> 5) == q).astype(F32).astype(dtype)


def to_rows(dtype=BF16):
    p, q = iota((TILE, TILE), 0), iota((TILE, TILE), 1)
    return ((q & 31) * PARTS + (q >> 5) == p).astype(F32).astype(dtype)


def dot(a, b):
    return jnp.dot(a, b, preferred_element_type=F32)


def pack_body(slots, first, half, experts, routes_ref, tokens_ref, out_ref, codes_ref, tok_ref):
    rows, width = out_ref.shape
    toks = tokens_ref.shape[0]
    step = pl.program_id(0)

    @pl.when(step == 0)
    def _():
        names = iota((experts, toks), 0)
        hits = jnp.zeros((experts, toks), F32)
        for k in range(routes_ref.shape[0]):
            hits = hits + (routes_ref[k : k + 1, :] == names).astype(F32)
        before = (iota((toks, toks), 0) < iota((toks, toks), 1)).astype(F32).astype(BF16)
        earlier = dot(hits.astype(BF16), before)
        codes = (hits * (earlier + 1.0)).astype(BF16)
        wide = (toks, PARTS * toks)
        spread = ((iota(wide, 1) & (toks - 1)) == iota(wide, 0)).astype(F32).astype(BF16)
        codes_ref[...] = dot(codes, spread).astype(BF16)
        for s in range(PARTS):
            tok_ref[s * toks : (s + 1) * toks, :] = tokens_ref[:, s * width : (s + 1) * width]

    most = pl.num_programs(0) * rows // PARTS
    row = step * rows + iota((rows, 1), 0)
    expert, rank = expert_and_rank(row >> 3, slots, first, half, 1024)
    del most
    named = (iota((rows, experts), 1) == expert).astype(F32).astype(BF16)
    found = dot(named, codes_ref[...])
    wide = (rows, PARTS * toks)
    want = jnp.where((iota(wide, 1) >> 6) == (row & (PARTS - 1)), (rank + 1).astype(F32), -1.0)
    picks = jnp.where(found == want, 1.0, 0.0).astype(BF16)
    out_ref[...] = dot(picks, tok_ref[...]).astype(BF16)


def pack(routes_t, tokens, slots, first, half, devices):
    toks, width = tokens.shape
    part = width // PARTS
    rows = devices * slots * PARTS
    block = 512
    experts = devices // 2
    return pl.pallas_call(
        functools.partial(pack_body, slots, first, half, experts),
        grid=(rows // block,),
        out_shape=jax.ShapeDtypeStruct((rows, part), BF16),
        in_specs=[
            pl.BlockSpec(routes_t.shape, lambda i: (0, 0)),
            pl.BlockSpec(tokens.shape, lambda i: (0, 0)),
        ],
        out_specs=pl.BlockSpec((block, part), lambda i: (i, 0)),
        scratch_shapes=[
            pltpu.VMEM((experts, PARTS * toks), BF16),
            pltpu.VMEM((PARTS * toks, part), BF16),
        ],
        compiler_params=pltpu.CompilerParams(vmem_limit_bytes=32 << 20),
        cost_estimate=pl.CostEstimate(
            flops=2 * rows * PARTS * toks * part, bytes_accessed=2 * rows * part, transcendentals=0
        ),
        name="pack",
    )(routes_t, tokens)


def ffn_body(blocks, rows_in, ga, gb, ua, ub, da, db, out_ref, parts, acc, hidden):
    step = pl.program_id(0)
    block, part = rows_in.shape
    tiles = block // TILE
    half = hidden.shape[1] // 2

    @pl.when(step < blocks)
    def _():
        order = to_parts()
        for t in range(tiles):
            turned = dot(order, rows_in[t * TILE : (t + 1) * TILE, :]).astype(BF16)
            at = pl.multiple_of((step * tiles + t) * 32, 32)
            for s in range(PARTS):
                parts[s, pl.ds(at, 32), :] = turned[s * 32 : (s + 1) * 32, :]

    def add(first):
        x = parts[jnp.where(first, 0, step - blocks)]
        for k, w in enumerate((ga, gb, ua, ub)):
            value = dot(x, w[0])
            acc[k] = value if first else acc[k] + value

    @pl.when(step == blocks)
    def _():
        add(True)

    @pl.when((step > blocks) & (step < blocks + PARTS))
    def _():
        add(False)

    @pl.when(step == blocks + PARTS - 1)
    def _():
        for k in range(2):
            gate = acc[k]
            value = gate / (1.0 + jnp.exp(-gate)) * acc[2 + k]
            hidden[:, k * half : (k + 1) * half] = value.astype(BF16)

    @pl.when((step >= blocks + PARTS) & (step < blocks + 2 * PARTS))
    def _():
        value = dot(hidden[:, :half], da[0]) + dot(hidden[:, half:], db[0])
        parts[step - blocks - PARTS] = value.astype(BF16)

    @pl.when(step >= blocks + 2 * PARTS)
    def _():
        order = to_rows()
        for t in range(tiles):
            at = pl.multiple_of(((step - blocks - 2 * PARTS) * tiles + t) * 32, 32)
            stacked = jnp.concatenate([parts[s, pl.ds(at, 32), :] for s in range(PARTS)], axis=0)
            out_ref[t * TILE : (t + 1) * TILE, :] = dot(order, stacked).astype(BF16)


def ffn(rows_in, gate, gate_other, up, up_other, down, down_other):
    total, part = rows_in.shape
    rows = total // PARTS
    half = gate.shape[2]
    block = 512
    blocks = total // block
    last = PARTS - 1
    into = lambda i: (0, jnp.clip(i - blocks, 0, last), 0)
    outof = lambda i: (0, 0, jnp.clip(i - blocks - PARTS, 0, last))
    up_spec = pl.BlockSpec((1, part, half), into)
    down_spec = pl.BlockSpec((1, half, part), outof)
    return pl.pallas_call(
        functools.partial(ffn_body, blocks),
        grid=(2 * blocks + 2 * PARTS,),
        out_shape=jax.ShapeDtypeStruct((total, part), BF16),
        in_specs=[
            pl.BlockSpec((block, part), lambda i: (jnp.minimum(i, blocks - 1), 0)),
            up_spec,
            up_spec,
            up_spec,
            up_spec,
            down_spec,
            down_spec,
        ],
        out_specs=pl.BlockSpec((block, part), lambda i: (jnp.maximum(i - blocks - 2 * PARTS, 0), 0)),
        scratch_shapes=[
            pltpu.VMEM((PARTS, rows, part), BF16),
            pltpu.VMEM((4, rows, half), F32),
            pltpu.VMEM((rows, 2 * half), BF16),
        ],
        compiler_params=pltpu.CompilerParams(vmem_limit_bytes=48 << 20),
        cost_estimate=pl.CostEstimate(
            flops=2 * rows * part * PARTS * half * 6,
            bytes_accessed=4 * total * part + 12 * part * PARTS * half,
            transcendentals=rows * 2 * half,
        ),
        name="experts",
    )(rows_in, gate, gate_other, up, up_other, down, down_other)


def mix_body(slots, first, half, experts, blocks, with_sum, *refs):
    if with_sum:
        routes_ref, gates_ref, rows_ref, sum_ref, out_ref, parts = refs
    else:
        routes_ref, gates_ref, rows_ref, out_ref, parts = refs
    step = pl.program_id(0)
    block, part = rows_ref.shape
    tiles = block // TILE
    toks = routes_ref.shape[0]
    order = to_parts()
    for t in range(tiles):
        turned = dot(order, rows_ref[t * TILE : (t + 1) * TILE, :]).astype(BF16)
        at = pl.multiple_of((step * tiles + t) * 32, 32)
        for s in range(PARTS):
            parts[s, pl.ds(at, 32), :] = turned[s * 32 : (s + 1) * 32, :]

    @pl.when(step == blocks - 1)
    def _():
        rows = parts.shape[1]
        names = iota((toks, experts), 1)
        hits = jnp.zeros((toks, experts), F32)
        weight = jnp.zeros((toks, experts), F32)
        for k in range(routes_ref.shape[1]):
            hit = (routes_ref[:, k : k + 1] == names).astype(F32)
            hits = hits + hit
            weight = weight + hit * gates_ref[:, k : k + 1]
        before = (iota((toks, toks), 1) < iota((toks, toks), 0)).astype(F32).astype(BF16)
        codes = (hits * (dot(before, hits.astype(BF16)) + 1.0)).astype(BF16)
        high = weight.astype(BF16)
        low = (weight - high.astype(F32)).astype(BF16)
        expert, rank = expert_and_rank(iota((1, rows), 1), slots, first, half, 1024)
        spread = (iota((experts, rows), 0) == expert).astype(F32).astype(BF16)
        here = dot(codes, spread) == (rank + 1).astype(F32)
        high = jnp.where(here, dot(high, spread), 0.0).astype(BF16)
        low = jnp.where(here, dot(low, spread), 0.0).astype(BF16)
        both = jnp.concatenate([high, low], axis=0)
        for s in range(PARTS):
            value = dot(both, parts[s])
            value = value[:toks] + value[toks:]
            at = slice(s * part, (s + 1) * part)
            if with_sum:
                value = value + sum_ref[:, at]
            out_ref[:, at] = value.astype(out_ref.dtype)


def mix(routes, gates, rows_in, so_far, slots, first, half, devices, dtype):
    total, part = rows_in.shape
    toks = routes.shape[0]
    block = 512
    blocks = total // block
    whole = lambda i: (0, 0)
    extra = () if so_far is None else (so_far,)
    return pl.pallas_call(
        functools.partial(mix_body, slots, first, half, devices // 2, blocks, bool(extra)),
        grid=(blocks,),
        out_shape=jax.ShapeDtypeStruct((toks, part * PARTS), dtype),
        in_specs=[
            pl.BlockSpec(routes.shape, whole),
            pl.BlockSpec(gates.shape, whole),
            pl.BlockSpec((block, part), lambda i: (i, 0)),
        ]
        + [pl.BlockSpec(x.shape, whole) for x in extra],
        out_specs=pl.BlockSpec((toks, part * PARTS), whole),
        scratch_shapes=[pltpu.VMEM((PARTS, total // PARTS, part), BF16)],
        compiler_params=pltpu.CompilerParams(vmem_limit_bytes=32 << 20),
        cost_estimate=pl.CostEstimate(
            flops=2 * total * TILE * part, bytes_accessed=2 * total * part, transcendentals=0
        ),
        name="mix",
    )(routes, gates, rows_in, *extra)


def exchange(rows, devices):
    part = rows.shape[1]
    rows = rows.reshape(devices, -1, part)
    return lax.all_to_all(rows, AXES, split_axis=0, concat_axis=0, tiled=True).reshape(-1, part)


def local(tokens, routes, gates, gate_weight, up_weight, down_weight):
    devices = lax.axis_size("group") * lax.axis_size("local")
    half = sum(SLOTS)
    swap = [(i, i ^ 1) for i in range(lax.axis_size("local"))]
    others = [lax.ppermute(w, "local", swap) for w in (gate_weight, up_weight, down_weight)]
    routes_t = routes.T
    firsts = [sum(SLOTS[:n]) for n in range(len(SLOTS))]
    packed = [pack(routes_t, tokens, n, f, half, devices) for n, f in zip(SLOTS, firsts)]
    arrived = [exchange(p, devices) for p in packed]
    done = [
        ffn(a, gate_weight, others[0], up_weight, others[1], down_weight, others[2])
        for a in arrived
    ]
    back = [exchange(d, devices) for d in done]
    mixed = None
    for at, (n, f) in enumerate(zip(SLOTS, firsts)):
        dtype = BF16 if at == len(SLOTS) - 1 else F32
        mixed = mix(routes, gates, back[at], mixed, n, f, half, devices, dtype)
    return mixed


def solution(mesh):
    placed = (
        P(AXES, None),
        P(AXES, None),
        P(AXES, None),
        P(AXES, None, None),
        P(AXES, None, None),
        P(AXES, None, None),
    )
    return jax.shard_map(
        local, mesh=mesh, in_specs=placed, out_specs=P(AXES, None), check_vma=False
    )
```

```python
import functools

import jax
import jax.numpy as jnp
from jax import lax
from jax.experimental import pallas as pl
from jax.experimental.pallas import tpu as pltpu
from jax.sharding import Mesh, PartitionSpec as P

AXES = ("group", "chip", "core")
CHIPS = ("group", "chip")
PARTS = 4
ROWS = 64
TILE = ROWS * PARTS
SLOTS = (6, 4)
BLOCK = 512
VMEM = 60 << 20
F32 = jnp.float32
BF16 = jnp.bfloat16


def quotient(value, by, most):
    shift = 0
    while True:
        factor = (1 << shift) // by + 1
        if factor * most < 1 << 31 and all(v * factor >> shift == v // by for v in range(most + 1)):
            return lax.shift_right_logical(value * factor, shift)
        shift += 1


def iota(shape, dim):
    return lax.broadcasted_iota(jnp.int32, shape, dim)


def expert_and_rank(row, slots, first):
    expert = quotient(row, slots, 1024)
    return expert, row - expert * slots + first


def order(rows_first):
    p, q = iota((TILE, TILE), rows_first), iota((TILE, TILE), 1 - rows_first)
    return (lax.rem(p, ROWS) * PARTS + lax.div(p, ROWS) == q).astype(F32).astype(BF16)


def dot(a, b):
    return jnp.dot(a, b, preferred_element_type=F32)


def pack_body(slots, first, experts, routes_ref, tokens_ref, out_ref, codes_ref, tok_ref):
    rows, width = out_ref.shape
    toks = tokens_ref.shape[0]
    step = pl.program_id(0)

    @pl.when(step == 0)
    def _():
        names = iota((experts, toks), 0)
        hits = jnp.zeros((experts, toks), F32)
        for k in range(routes_ref.shape[0]):
            hits = hits + (routes_ref[k : k + 1, :] == names).astype(F32)
        before = (iota((toks, toks), 0) < iota((toks, toks), 1)).astype(F32).astype(BF16)
        earlier = dot(hits.astype(BF16), before)
        codes = (hits * (earlier + 1.0)).astype(BF16)
        wide = (toks, PARTS * toks)
        spread = ((iota(wide, 1) & (toks - 1)) == iota(wide, 0)).astype(F32).astype(BF16)
        codes_ref[...] = dot(codes, spread).astype(BF16)
        for s in range(PARTS):
            tok_ref[s * toks : (s + 1) * toks, :] = tokens_ref[:, s * width : (s + 1) * width]

    row = step * rows + iota((rows, 1), 0)
    expert, rank = expert_and_rank(lax.div(row, PARTS), slots, first)
    named = (iota((rows, experts), 1) == expert).astype(F32).astype(BF16)
    found = dot(named, codes_ref[...])
    wide = (rows, PARTS * toks)
    want = jnp.where(lax.div(iota(wide, 1), toks) == lax.rem(row, PARTS), (rank + 1).astype(F32), -1.0)
    picks = jnp.where(found == want, 1.0, 0.0).astype(BF16)
    out_ref[...] = dot(picks, tok_ref[...]).astype(BF16)


def pack(routes_t, tokens, slots, first, experts):
    toks, width = tokens.shape
    part = width // PARTS
    rows = experts * slots * PARTS
    block = BLOCK
    return pl.pallas_call(
        functools.partial(pack_body, slots, first, experts),
        grid=(rows // block,),
        out_shape=jax.ShapeDtypeStruct((rows, part), BF16),
        in_specs=[
            pl.BlockSpec(routes_t.shape, lambda i: (0, 0)),
            pl.BlockSpec(tokens.shape, lambda i: (0, 0)),
        ],
        out_specs=pl.BlockSpec((block, part), lambda i: (i, 0)),
        scratch_shapes=[
            pltpu.VMEM((experts, PARTS * toks), BF16),
            pltpu.VMEM((PARTS * toks, part), BF16),
        ],
        compiler_params=pltpu.CompilerParams(vmem_limit_bytes=VMEM),
        cost_estimate=pl.CostEstimate(
            flops=2 * rows * PARTS * toks * part, bytes_accessed=2 * rows * part, transcendentals=0
        ),
        name="pack",
    )(routes_t, tokens)


def split(step, rows_ref, parts):
    apart = order(0)
    tiles = rows_ref.shape[0] // TILE
    for t in range(tiles):
        turned = dot(apart, rows_ref[t * TILE : (t + 1) * TILE, :]).astype(BF16)
        at = pl.multiple_of((step * tiles + t) * ROWS, ROWS)
        for s in range(PARTS):
            parts[s, pl.ds(at, ROWS), :] = turned[s * ROWS : (s + 1) * ROWS, :]


def ffn_body(blocks, rows_in, ga, gb, ua, ub, da, db, out_ref, parts, acc, hidden):
    step = pl.program_id(0)
    block = rows_in.shape[0]
    half = hidden.shape[1] // 2

    @pl.when(step < blocks)
    def _():
        split(step, rows_in, parts)

    def add(first):
        x = parts[jnp.where(first, 0, step - blocks)]
        for k, w in enumerate((ga, gb, ua, ub)):
            value = dot(x, w[0])
            acc[k] = value if first else acc[k] + value

    @pl.when(step == blocks)
    def _():
        add(True)

    @pl.when((step > blocks) & (step < blocks + PARTS))
    def _():
        add(False)

    @pl.when(step == blocks + PARTS - 1)
    def _():
        for k in range(2):
            gate = acc[k]
            value = gate / (1.0 + jnp.exp(-gate)) * acc[2 + k]
            hidden[:, k * half : (k + 1) * half] = value.astype(BF16)

    @pl.when((step >= blocks + PARTS) & (step < blocks + 2 * PARTS))
    def _():
        halves = [dot(hidden[:, :half], da[0]), dot(hidden[:, half:], db[0])]
        own, other = (v.astype(BF16).astype(F32) for v in halves)
        parts[step - blocks - PARTS] = (own + other).astype(BF16)

    @pl.when(step >= blocks + 2 * PARTS)
    def _():
        back = order(1)
        tiles = block // TILE
        for t in range(tiles):
            at = pl.multiple_of(((step - blocks - 2 * PARTS) * tiles + t) * ROWS, ROWS)
            stacked = jnp.concatenate([parts[s, pl.ds(at, ROWS), :] for s in range(PARTS)], axis=0)
            out_ref[t * TILE : (t + 1) * TILE, :] = dot(back, stacked).astype(BF16)


def ffn(rows_in, gate, gate_other, up, up_other, down, down_other):
    total, part = rows_in.shape
    rows = total // PARTS
    half = gate.shape[2]
    block = BLOCK
    blocks = total // block
    last = PARTS - 1
    into = lambda i: (0, jnp.clip(i - blocks, 0, last), 0)
    outof = lambda i: (0, 0, jnp.clip(i - blocks - PARTS, 0, last))
    up_spec = pl.BlockSpec((1, part, half), into)
    down_spec = pl.BlockSpec((1, half, part), outof)
    return pl.pallas_call(
        functools.partial(ffn_body, blocks),
        grid=(2 * blocks + 2 * PARTS,),
        out_shape=jax.ShapeDtypeStruct((total, part), BF16),
        in_specs=[
            pl.BlockSpec((block, part), lambda i: (jnp.minimum(i, blocks - 1), 0)),
            up_spec,
            up_spec,
            up_spec,
            up_spec,
            down_spec,
            down_spec,
        ],
        out_specs=pl.BlockSpec((block, part), lambda i: (jnp.maximum(i - blocks - 2 * PARTS, 0), 0)),
        scratch_shapes=[
            pltpu.VMEM((PARTS, rows, part), BF16),
            pltpu.VMEM((4, rows, half), F32),
            pltpu.VMEM((rows, 2 * half), BF16),
        ],
        compiler_params=pltpu.CompilerParams(vmem_limit_bytes=VMEM),
        cost_estimate=pl.CostEstimate(
            flops=2 * rows * part * PARTS * half * 6,
            bytes_accessed=4 * total * part + 12 * part * PARTS * half,
            transcendentals=rows * 2 * half,
        ),
        name="experts",
    )(rows_in, gate, gate_other, up, up_other, down, down_other)


def mix_body(slots, first, experts, blocks, with_sum, *refs):
    if with_sum:
        routes_ref, gates_ref, rows_ref, sum_ref, out_ref, parts = refs
    else:
        routes_ref, gates_ref, rows_ref, out_ref, parts = refs
    step = pl.program_id(0)
    part = rows_ref.shape[1]
    toks = routes_ref.shape[0]
    split(step, rows_ref, parts)

    @pl.when(step == blocks - 1)
    def _():
        rows = parts.shape[1]
        names = iota((toks, experts), 1)
        hits = jnp.zeros((toks, experts), F32)
        weight = jnp.zeros((toks, experts), F32)
        for k in range(routes_ref.shape[1]):
            hit = (routes_ref[:, k : k + 1] == names).astype(F32)
            hits = hits + hit
            weight = weight + hit * gates_ref[:, k : k + 1]
        before = (iota((toks, toks), 1) < iota((toks, toks), 0)).astype(F32).astype(BF16)
        codes = (hits * (dot(before, hits.astype(BF16)) + 1.0)).astype(BF16)
        high = weight.astype(BF16)
        low = (weight - high.astype(F32)).astype(BF16)
        expert, rank = expert_and_rank(iota((1, rows), 1), slots, first)
        spread = (iota((experts, rows), 0) == expert).astype(F32).astype(BF16)
        here = dot(codes, spread) == (rank + 1).astype(F32)
        high = jnp.where(here, dot(high, spread), 0.0).astype(BF16)
        low = jnp.where(here, dot(low, spread), 0.0).astype(BF16)
        both = jnp.concatenate([high, low], axis=0)
        for s in range(PARTS):
            value = dot(both, parts[s])
            value = value[:toks] + value[toks:]
            at = slice(s * part, (s + 1) * part)
            if with_sum:
                value = value + sum_ref[:, at]
            out_ref[:, at] = value.astype(out_ref.dtype)


def mix(routes, gates, rows_in, so_far, slots, first, experts, dtype):
    total, part = rows_in.shape
    toks = routes.shape[0]
    block = BLOCK
    blocks = total // block
    whole = lambda i: (0, 0)
    extra = () if so_far is None else (so_far,)
    return pl.pallas_call(
        functools.partial(mix_body, slots, first, experts, blocks, bool(extra)),
        grid=(blocks,),
        out_shape=jax.ShapeDtypeStruct((toks, part * PARTS), dtype),
        in_specs=[
            pl.BlockSpec(routes.shape, whole),
            pl.BlockSpec(gates.shape, whole),
            pl.BlockSpec((block, part), lambda i: (i, 0)),
        ]
        + [pl.BlockSpec(x.shape, whole) for x in extra],
        out_specs=pl.BlockSpec((toks, part * PARTS), whole),
        scratch_shapes=[pltpu.VMEM((PARTS, total // PARTS, part), BF16)],
        compiler_params=pltpu.CompilerParams(vmem_limit_bytes=VMEM),
        cost_estimate=pl.CostEstimate(
            flops=2 * total * TILE * part, bytes_accessed=2 * total * part, transcendentals=0
        ),
        name="mix",
    )(routes, gates, rows_in, *extra)


def exchange(rows, experts):
    part = rows.shape[1]
    rows = rows.reshape(experts, -1, part)
    return lax.all_to_all(rows, CHIPS, split_axis=0, concat_axis=0, tiled=True).reshape(-1, part)


def local(tokens, routes, gates, gate_weight, up_weight, down_weight):
    experts = lax.axis_size("group") * lax.axis_size("chip")
    swap = [(0, 1), (1, 0)]
    others = [lax.ppermute(w, "core", swap) for w in (gate_weight, up_weight, down_weight)]
    routes_t = routes.T
    firsts = [sum(SLOTS[:n]) for n in range(len(SLOTS))]
    packed = [pack(routes_t, tokens, n, f, experts) for n, f in zip(SLOTS, firsts)]
    arrived = [exchange(p, experts) for p in packed]
    done = [
        ffn(a, gate_weight, others[0], up_weight, others[1], down_weight, others[2])
        for a in arrived
    ]
    back = [exchange(d, experts) for d in done]
    mixed = None
    for at, (n, f) in enumerate(zip(SLOTS, firsts)):
        dtype = BF16 if at == len(SLOTS) - 1 else F32
        mixed = mix(routes, gates, back[at], mixed, n, f, experts, dtype)
    return mixed


def solution(mesh):
    groups, members = mesh.devices.shape
    by_core = Mesh(mesh.devices.reshape(groups, members // 2, 2), AXES)
    placed = (
        P(AXES, None),
        P(AXES, None),
        P(AXES, None),
        P(AXES, None, None),
        P(AXES, None, None),
        P(AXES, None, None),
    )
    return jax.shard_map(
        local, mesh=by_core, in_specs=placed, out_specs=P(AXES, None), check_vma=False
    )
```

```python
import functools

import jax
import jax.numpy as jnp
from jax import lax
from jax.experimental import pallas as pl
from jax.experimental.pallas import tpu as pltpu
from jax.sharding import Mesh, PartitionSpec as P

AXES = ("group", "chip", "core")
CHIPS = ("group", "chip")
PARTS = 4
ROWS = 64
TILE = ROWS * PARTS
SLOTS = (6, 4)
BLOCK = 512
VMEM = 60 << 20
SMALL = 20 << 20
F32 = jnp.float32
BF16 = jnp.bfloat16


def quotient(value, by, most):
    shift = 0
    while True:
        factor = (1 << shift) // by + 1
        if factor * most < 1 << 31 and all(v * factor >> shift == v // by for v in range(most + 1)):
            return lax.shift_right_logical(value * factor, shift)
        shift += 1


def iota(shape, dim):
    return lax.broadcasted_iota(jnp.int32, shape, dim)


def expert_and_rank(row, slots, first):
    expert = quotient(row, slots, 1024)
    return expert, row - expert * slots + first


def order(rows_first):
    p, q = iota((TILE, TILE), rows_first), iota((TILE, TILE), 1 - rows_first)
    return (lax.rem(p, ROWS) * PARTS + lax.div(p, ROWS) == q).astype(F32).astype(BF16)


def dot(a, b):
    return jnp.dot(a, b, preferred_element_type=F32)


def pack_body(slots, first, routes_ref, tokens_ref, out_ref, tok_ref, ready, sems):
    toks = routes_ref.shape[1]
    total, width = ready.shape
    experts = total // (slots * PARTS)
    for s in range(PARTS):
        tok_ref[s * toks : (s + 1) * toks, :] = tokens_ref[:, s * width : (s + 1) * width]
    names = iota((experts, toks), 0)
    hits = jnp.zeros((experts, toks), F32)
    for k in range(routes_ref.shape[0]):
        hits = hits + (routes_ref[k : k + 1, :] == names).astype(F32)
    before = (iota((toks, toks), 0) < iota((toks, toks), 1)).astype(F32).astype(BF16)
    earlier = dot(hits.astype(BF16), before)
    codes = (hits * (earlier + 1.0)).astype(BF16)
    codes = jnp.concatenate([codes] * PARTS, axis=1)
    copies = []
    for n in range(total // BLOCK):
        at = slice(n * BLOCK, (n + 1) * BLOCK)
        row = n * BLOCK + iota((BLOCK, 1), 0)
        expert, rank = expert_and_rank(lax.div(row, PARTS), slots, first)
        named = (iota((BLOCK, experts), 1) == expert).astype(F32).astype(BF16)
        found = dot(named, codes)
        wide = (BLOCK, PARTS * toks)
        want = jnp.where(lax.div(iota(wide, 1), toks) == lax.rem(row, PARTS), (rank + 1).astype(F32), -1.0)
        picks = jnp.where(found == want, 1.0, 0.0).astype(BF16)
        ready[at, :] = dot(picks, tok_ref[...]).astype(BF16)
        copies.append(pltpu.make_async_copy(ready.at[at, :], out_ref.at[at, :], sems.at[n]))
        copies[-1].start()
    for copy in copies:
        copy.wait()


def pack(routes_t, tokens, slots, first, experts):
    toks, width = tokens.shape
    part = width // PARTS
    rows = experts * slots * PARTS
    return pl.pallas_call(
        functools.partial(pack_body, slots, first),
        out_shape=jax.ShapeDtypeStruct((rows, part), BF16),
        in_specs=[pl.BlockSpec(memory_space=pltpu.VMEM)] * 2,
        out_specs=pl.BlockSpec(memory_space=pl.ANY),
        scratch_shapes=[
            pltpu.VMEM((PARTS * toks, part), BF16),
            pltpu.VMEM((rows, part), BF16),
            pltpu.SemaphoreType.DMA((rows // BLOCK,)),
        ],
        compiler_params=pltpu.CompilerParams(vmem_limit_bytes=VMEM),
        cost_estimate=pl.CostEstimate(
            flops=2 * rows * PARTS * toks * part, bytes_accessed=2 * rows * part, transcendentals=0
        ),
        name="pack",
    )(routes_t, tokens)


def split(step, rows_ref, parts):
    apart = order(0)
    tiles = rows_ref.shape[0] // TILE
    for t in range(tiles):
        turned = dot(apart, rows_ref[t * TILE : (t + 1) * TILE, :]).astype(BF16)
        at = pl.multiple_of((step * tiles + t) * ROWS, ROWS)
        for s in range(PARTS):
            parts[s, pl.ds(at, ROWS), :] = turned[s * ROWS : (s + 1) * ROWS, :]


def ffn_body(blocks, rows_in, ga, gb, ua, ub, da, db, out_ref, parts, acc, hidden):
    step = pl.program_id(0)
    block = rows_in.shape[0]
    half = hidden.shape[1] // 2

    @pl.when(step < blocks)
    def _():
        split(step, rows_in, parts)

    def add(first):
        x = parts[jnp.where(first, 0, step - blocks)]
        for k, w in enumerate((ga, gb, ua, ub)):
            value = dot(x, w[0])
            acc[k] = value if first else acc[k] + value

    @pl.when(step == blocks)
    def _():
        add(True)

    @pl.when((step > blocks) & (step < blocks + PARTS))
    def _():
        add(False)

    @pl.when(step == blocks + PARTS - 1)
    def _():
        for k in range(2):
            gate = acc[k]
            value = gate / (1.0 + jnp.exp(-gate)) * acc[2 + k]
            hidden[:, k * half : (k + 1) * half] = value.astype(BF16)

    @pl.when((step >= blocks + PARTS) & (step < blocks + 2 * PARTS))
    def _():
        halves = [dot(hidden[:, :half], da[0]), dot(hidden[:, half:], db[0])]
        own, other = (v.astype(BF16).astype(F32) for v in halves)
        parts[step - blocks - PARTS] = (own + other).astype(BF16)

    @pl.when(step >= blocks + 2 * PARTS)
    def _():
        back = order(1)
        tiles = block // TILE
        for t in range(tiles):
            at = pl.multiple_of(((step - blocks - 2 * PARTS) * tiles + t) * ROWS, ROWS)
            stacked = jnp.concatenate([parts[s, pl.ds(at, ROWS), :] for s in range(PARTS)], axis=0)
            out_ref[t * TILE : (t + 1) * TILE, :] = dot(back, stacked).astype(BF16)


def ffn(rows_in, gate, gate_other, up, up_other, down, down_other):
    total, part = rows_in.shape
    rows = total // PARTS
    half = gate.shape[2]
    block = BLOCK
    blocks = total // block
    last = PARTS - 1
    into = lambda i: (0, jnp.clip(i - blocks, 0, last), 0)
    outof = lambda i: (0, 0, jnp.clip(i - blocks - PARTS, 0, last))
    up_spec = pl.BlockSpec((1, part, half), into)
    down_spec = pl.BlockSpec((1, half, part), outof)
    return pl.pallas_call(
        functools.partial(ffn_body, blocks),
        grid=(2 * blocks + 2 * PARTS,),
        out_shape=jax.ShapeDtypeStruct((total, part), BF16),
        in_specs=[
            pl.BlockSpec((block, part), lambda i: (jnp.minimum(i, blocks - 1), 0)),
            up_spec,
            up_spec,
            up_spec,
            up_spec,
            down_spec,
            down_spec,
        ],
        out_specs=pl.BlockSpec((block, part), lambda i: (jnp.maximum(i - blocks - 2 * PARTS, 0), 0)),
        scratch_shapes=[
            pltpu.VMEM((PARTS, rows, part), BF16),
            pltpu.VMEM((4, rows, half), F32),
            pltpu.VMEM((rows, 2 * half), BF16),
        ],
        compiler_params=pltpu.CompilerParams(vmem_limit_bytes=VMEM),
        cost_estimate=pl.CostEstimate(
            flops=2 * rows * part * PARTS * half * 6,
            bytes_accessed=4 * total * part + 12 * part * PARTS * half,
            transcendentals=rows * 2 * half,
        ),
        name="experts",
    )(rows_in, gate, gate_other, up, up_other, down, down_other)


def plan_body(chunks, experts, routes_ref, gates_ref, *outs):
    toks = routes_ref.shape[0]
    names = iota((toks, experts), 1)
    hits = jnp.zeros((toks, experts), F32)
    weight = jnp.zeros((toks, experts), F32)
    for k in range(routes_ref.shape[1]):
        hit = (routes_ref[:, k : k + 1] == names).astype(F32)
        hits = hits + hit
        weight = weight + hit * gates_ref[:, k : k + 1]
    before = (iota((toks, toks), 1) < iota((toks, toks), 0)).astype(F32).astype(BF16)
    codes = (hits * (dot(before, hits.astype(BF16)) + 1.0)).astype(BF16)
    high = weight.astype(BF16)
    low = (weight - high.astype(F32)).astype(BF16)
    for (slots, first), out_ref in zip(chunks, outs):
        rows = out_ref.shape[1]
        expert, rank = expert_and_rank(iota((1, rows), 1), slots, first)
        spread = (iota((experts, rows), 0) == expert).astype(F32).astype(BF16)
        here = dot(codes, spread) == (rank + 1).astype(F32)
        for h, half in enumerate((high, low)):
            placed = jnp.where(here, dot(half, spread), 0.0)
            out_ref[h * toks : (h + 1) * toks, :] = placed.astype(BF16)


def plan(routes, gates, chunks, experts):
    toks = routes.shape[0]
    sizes = [experts * n for n, _ in chunks]
    return pl.pallas_call(
        functools.partial(plan_body, chunks, experts),
        out_shape=[jax.ShapeDtypeStruct((2 * toks, size), BF16) for size in sizes],
        compiler_params=pltpu.CompilerParams(vmem_limit_bytes=SMALL),
        cost_estimate=pl.CostEstimate(
            flops=6 * toks * experts * sum(sizes), bytes_accessed=4 * toks * sum(sizes), transcendentals=0
        ),
        name="plan",
    )(routes, gates)


def mix_body(weights_ref, rows_hbm, *refs):
    sum_ref, out_hbm, rows_ref, parts, result, in_sems, out_sems = refs if len(refs) == 7 else (None, *refs)
    total, part = rows_ref.shape
    toks = result.shape[0]
    arrivals = []
    for n in range(total // BLOCK):
        at = slice(n * BLOCK, (n + 1) * BLOCK)
        arrivals.append(pltpu.make_async_copy(rows_hbm.at[at, :], rows_ref.at[at, :], in_sems.at[n]))
        arrivals[-1].start()
    for n, arrival in enumerate(arrivals):
        arrival.wait()
        split(n, rows_ref.at[n * BLOCK : (n + 1) * BLOCK, :], parts)
    departures = []
    for s in range(PARTS):
        value = dot(weights_ref[...], parts[s])
        value = value[:toks] + value[toks:]
        at = slice(s * part, (s + 1) * part)
        if sum_ref is not None:
            value = value + sum_ref[:, at]
        result[:, at] = value.astype(result.dtype)
        departures.append(pltpu.make_async_copy(result.at[:, at], out_hbm.at[:, at], out_sems.at[s]))
        departures[-1].start()
    for departure in departures:
        departure.wait()


def mix(weights, rows_in, so_far, dtype):
    total, part = rows_in.shape
    toks = weights.shape[0] // 2
    here = pl.BlockSpec(memory_space=pltpu.VMEM)
    extra = () if so_far is None else (so_far,)
    return pl.pallas_call(
        mix_body,
        out_shape=jax.ShapeDtypeStruct((toks, part * PARTS), dtype),
        in_specs=[here, pl.BlockSpec(memory_space=pl.ANY)] + [here for _ in extra],
        out_specs=pl.BlockSpec(memory_space=pl.ANY),
        scratch_shapes=[
            pltpu.VMEM((total, part), BF16),
            pltpu.VMEM((PARTS, total // PARTS, part), BF16),
            pltpu.VMEM((toks, part * PARTS), dtype),
            pltpu.SemaphoreType.DMA((total // BLOCK,)),
            pltpu.SemaphoreType.DMA((PARTS,)),
        ],
        compiler_params=pltpu.CompilerParams(vmem_limit_bytes=SMALL),
        cost_estimate=pl.CostEstimate(
            flops=2 * total * TILE * part, bytes_accessed=2 * total * part, transcendentals=0
        ),
        name="mix",
    )(weights, rows_in, *extra)


def exchange(rows, experts):
    part = rows.shape[1]
    rows = rows.reshape(experts, -1, part)
    return lax.all_to_all(rows, CHIPS, split_axis=0, concat_axis=0, tiled=True).reshape(-1, part)


def local(tokens, routes, gates, gate_weight, up_weight, down_weight):
    experts = lax.axis_size("group") * lax.axis_size("chip")
    swap = [(0, 1), (1, 0)]
    others = [lax.ppermute(w, "core", swap) for w in (gate_weight, up_weight, down_weight)]
    routes_t = routes.T
    firsts = [sum(SLOTS[:n]) for n in range(len(SLOTS))]
    packed = [pack(routes_t, tokens, n, f, experts) for n, f in zip(SLOTS, firsts)]
    arrived = [exchange(p, experts) for p in packed]
    done = [
        ffn(a, gate_weight, others[0], up_weight, others[1], down_weight, others[2])
        for a in arrived
    ]
    back = [exchange(d, experts) for d in done]
    mixed = None
    for at, weights in enumerate(plan(routes, gates, tuple(zip(SLOTS, firsts)), experts)):
        mixed = mix(weights, back[at], mixed, BF16 if at == len(SLOTS) - 1 else F32)
    return mixed


def solution(mesh):
    groups, members = mesh.devices.shape
    by_core = Mesh(mesh.devices.reshape(groups, members // 2, 2), AXES)
    placed = (
        P(AXES, None),
        P(AXES, None),
        P(AXES, None),
        P(AXES, None, None),
        P(AXES, None, None),
        P(AXES, None, None),
    )
    return jax.shard_map(
        local, mesh=by_core, in_specs=placed, out_specs=P(AXES, None), check_vma=False
    )
```

```python
import functools

import jax
import jax.numpy as jnp
from jax import lax
from jax.experimental import pallas as pl
from jax.experimental.pallas import tpu as pltpu
from jax.sharding import Mesh, PartitionSpec as P

AXES = ("group", "chip", "core")
CHIPS = ("group", "chip")
PARTS = 4
ROWS = 64
TILE = ROWS * PARTS
SLOTS = (4, 6)
BLOCK = 512
VMEM = 60 << 20
SMALL = 20 << 20
F32 = jnp.float32
BF16 = jnp.bfloat16


def quotient(value, by, most):
    shift = 0
    while True:
        factor = (1 << shift) // by + 1
        if factor * most < 1 << 31 and all(v * factor >> shift == v // by for v in range(most + 1)):
            return lax.shift_right_logical(value * factor, shift)
        shift += 1


def iota(shape, dim):
    return lax.broadcasted_iota(jnp.int32, shape, dim)


def expert_and_rank(row, slots, first):
    expert = quotient(row, slots, 1024)
    return expert, row - expert * slots + first


def order(rows_first):
    p, q = iota((TILE, TILE), rows_first), iota((TILE, TILE), 1 - rows_first)
    return (lax.rem(p, ROWS) * PARTS + lax.div(p, ROWS) == q).astype(F32).astype(BF16)


def dot(a, b):
    return jnp.dot(a, b, preferred_element_type=F32)


def pack_body(slots, first, routes_ref, tokens_ref, out_ref, tok_ref, ready, sems):
    toks = routes_ref.shape[1]
    total, width = ready.shape
    experts = total // (slots * PARTS)
    for s in range(PARTS):
        tok_ref[s * toks : (s + 1) * toks, :] = tokens_ref[:, s * width : (s + 1) * width]
    names = iota((experts, toks), 0)
    hits = jnp.zeros((experts, toks), F32)
    for k in range(routes_ref.shape[0]):
        hits = hits + (routes_ref[k : k + 1, :] == names).astype(F32)
    before = (iota((toks, toks), 0) < iota((toks, toks), 1)).astype(F32).astype(BF16)
    earlier = dot(hits.astype(BF16), before)
    codes = (hits * (earlier + 1.0)).astype(BF16)
    codes = jnp.concatenate([codes] * PARTS, axis=1)
    copies = []
    for n in range(total // BLOCK):
        at = slice(n * BLOCK, (n + 1) * BLOCK)
        row = n * BLOCK + iota((BLOCK, 1), 0)
        expert, rank = expert_and_rank(lax.div(row, PARTS), slots, first)
        named = (iota((BLOCK, experts), 1) == expert).astype(F32).astype(BF16)
        found = dot(named, codes)
        wide = (BLOCK, PARTS * toks)
        want = jnp.where(lax.div(iota(wide, 1), toks) == lax.rem(row, PARTS), (rank + 1).astype(F32), -1.0)
        picks = jnp.where(found == want, 1.0, 0.0).astype(BF16)
        ready[at, :] = dot(picks, tok_ref[...]).astype(BF16)
        copies.append(pltpu.make_async_copy(ready.at[at, :], out_ref.at[at, :], sems.at[n]))
        copies[-1].start()
    for copy in copies:
        copy.wait()


def pack(routes_t, tokens, slots, first, experts):
    toks, width = tokens.shape
    part = width // PARTS
    rows = experts * slots * PARTS
    return pl.pallas_call(
        functools.partial(pack_body, slots, first),
        out_shape=jax.ShapeDtypeStruct((rows, part), BF16),
        in_specs=[pl.BlockSpec(memory_space=pltpu.VMEM)] * 2,
        out_specs=pl.BlockSpec(memory_space=pl.ANY),
        scratch_shapes=[
            pltpu.VMEM((PARTS * toks, part), BF16),
            pltpu.VMEM((rows, part), BF16),
            pltpu.SemaphoreType.DMA((rows // BLOCK,)),
        ],
        compiler_params=pltpu.CompilerParams(vmem_limit_bytes=VMEM),
        cost_estimate=pl.CostEstimate(
            flops=2 * rows * PARTS * toks * part, bytes_accessed=2 * rows * part, transcendentals=0
        ),
        name="pack",
    )(routes_t, tokens)


def split(step, rows_ref, parts):
    apart = order(0)
    tiles = rows_ref.shape[0] // TILE
    for t in range(tiles):
        turned = dot(apart, rows_ref[t * TILE : (t + 1) * TILE, :]).astype(BF16)
        at = pl.multiple_of((step * tiles + t) * ROWS, ROWS)
        for s in range(PARTS):
            parts[s, pl.ds(at, ROWS), :] = turned[s * ROWS : (s + 1) * ROWS, :]


def ffn_body(blocks, rows_in, ga, gb, ua, ub, da, db, out_ref, parts, acc, hidden):
    step = pl.program_id(0)
    block = rows_in.shape[0]
    half = hidden.shape[1] // 2

    @pl.when(step < blocks)
    def _():
        split(step, rows_in, parts)

    def add(first):
        x = parts[jnp.where(first, 0, step - blocks)]
        for k, w in enumerate((ga, gb, ua, ub)):
            value = dot(x, w[0])
            acc[k] = value if first else acc[k] + value

    @pl.when(step == blocks)
    def _():
        add(True)

    @pl.when((step > blocks) & (step < blocks + PARTS))
    def _():
        add(False)

    @pl.when(step == blocks + PARTS - 1)
    def _():
        for k in range(2):
            gate = acc[k]
            value = gate / (1.0 + jnp.exp(-gate)) * acc[2 + k]
            hidden[:, k * half : (k + 1) * half] = value.astype(BF16)

    @pl.when((step >= blocks + PARTS) & (step < blocks + 2 * PARTS))
    def _():
        halves = [dot(hidden[:, :half], da[0]), dot(hidden[:, half:], db[0])]
        own, other = (v.astype(BF16).astype(F32) for v in halves)
        parts[step - blocks - PARTS] = (own + other).astype(BF16)

    @pl.when(step >= blocks + 2 * PARTS)
    def _():
        back = order(1)
        tiles = block // TILE
        for t in range(tiles):
            at = pl.multiple_of(((step - blocks - 2 * PARTS) * tiles + t) * ROWS, ROWS)
            stacked = jnp.concatenate([parts[s, pl.ds(at, ROWS), :] for s in range(PARTS)], axis=0)
            out_ref[t * TILE : (t + 1) * TILE, :] = dot(back, stacked).astype(BF16)


def ffn(rows_in, gate, gate_other, up, up_other, down, down_other):
    total, part = rows_in.shape
    rows = total // PARTS
    half = gate.shape[2]
    block = BLOCK
    blocks = total // block
    last = PARTS - 1
    into = lambda i: (0, jnp.clip(i - blocks, 0, last), 0)
    outof = lambda i: (0, 0, jnp.clip(i - blocks - PARTS, 0, last))
    up_spec = pl.BlockSpec((1, part, half), into)
    down_spec = pl.BlockSpec((1, half, part), outof)
    return pl.pallas_call(
        functools.partial(ffn_body, blocks),
        grid=(2 * blocks + 2 * PARTS,),
        out_shape=jax.ShapeDtypeStruct((total, part), BF16),
        in_specs=[
            pl.BlockSpec((block, part), lambda i: (jnp.minimum(i, blocks - 1), 0)),
            up_spec,
            up_spec,
            up_spec,
            up_spec,
            down_spec,
            down_spec,
        ],
        out_specs=pl.BlockSpec((block, part), lambda i: (jnp.maximum(i - blocks - 2 * PARTS, 0), 0)),
        scratch_shapes=[
            pltpu.VMEM((PARTS, rows, part), BF16),
            pltpu.VMEM((4, rows, half), F32),
            pltpu.VMEM((rows, 2 * half), BF16),
        ],
        compiler_params=pltpu.CompilerParams(vmem_limit_bytes=VMEM),
        cost_estimate=pl.CostEstimate(
            flops=2 * rows * part * PARTS * half * 6,
            bytes_accessed=4 * total * part + 12 * part * PARTS * half,
            transcendentals=rows * 2 * half,
        ),
        name="experts",
    )(rows_in, gate, gate_other, up, up_other, down, down_other)


def plan_body(chunks, experts, routes_ref, gates_ref, *outs):
    toks = routes_ref.shape[0]
    names = iota((toks, experts), 1)
    hits = jnp.zeros((toks, experts), F32)
    weight = jnp.zeros((toks, experts), F32)
    for k in range(routes_ref.shape[1]):
        hit = (routes_ref[:, k : k + 1] == names).astype(F32)
        hits = hits + hit
        weight = weight + hit * gates_ref[:, k : k + 1]
    before = (iota((toks, toks), 1) < iota((toks, toks), 0)).astype(F32).astype(BF16)
    codes = (hits * (dot(before, hits.astype(BF16)) + 1.0)).astype(BF16)
    high = weight.astype(BF16)
    low = (weight - high.astype(F32)).astype(BF16)
    for (slots, first), out_ref in zip(chunks, outs):
        rows = out_ref.shape[1]
        expert, rank = expert_and_rank(iota((1, rows), 1), slots, first)
        spread = (iota((experts, rows), 0) == expert).astype(F32).astype(BF16)
        here = dot(codes, spread) == (rank + 1).astype(F32)
        for h, half in enumerate((high, low)):
            placed = jnp.where(here, dot(half, spread), 0.0)
            out_ref[h * toks : (h + 1) * toks, :] = placed.astype(BF16)


def plan(routes, gates, chunks, experts):
    toks = routes.shape[0]
    sizes = [experts * n for n, _ in chunks]
    return pl.pallas_call(
        functools.partial(plan_body, chunks, experts),
        out_shape=[jax.ShapeDtypeStruct((2 * toks, size), BF16) for size in sizes],
        compiler_params=pltpu.CompilerParams(vmem_limit_bytes=SMALL),
        cost_estimate=pl.CostEstimate(
            flops=6 * toks * experts * sum(sizes), bytes_accessed=4 * toks * sum(sizes), transcendentals=0
        ),
        name="plan",
    )(routes, gates)


def mix_body(weights_ref, rows_hbm, *refs):
    sum_ref, out_hbm, rows_ref, parts, result, in_sems, out_sems = refs if len(refs) == 7 else (None, *refs)
    total, part = rows_ref.shape
    toks = result.shape[0]
    arrivals = []
    for n in range(total // BLOCK):
        at = slice(n * BLOCK, (n + 1) * BLOCK)
        arrivals.append(pltpu.make_async_copy(rows_hbm.at[at, :], rows_ref.at[at, :], in_sems.at[n]))
        arrivals[-1].start()
    for n, arrival in enumerate(arrivals):
        arrival.wait()
        split(n, rows_ref.at[n * BLOCK : (n + 1) * BLOCK, :], parts)
    departures = []
    for s in range(PARTS):
        value = dot(weights_ref[...], parts[s])
        value = value[:toks] + value[toks:]
        at = slice(s * part, (s + 1) * part)
        if sum_ref is not None:
            value = value + sum_ref[:, at]
        result[:, at] = value.astype(result.dtype)
        departures.append(pltpu.make_async_copy(result.at[:, at], out_hbm.at[:, at], out_sems.at[s]))
        departures[-1].start()
    for departure in departures:
        departure.wait()


def mix(weights, rows_in, so_far, dtype):
    total, part = rows_in.shape
    toks = weights.shape[0] // 2
    here = pl.BlockSpec(memory_space=pltpu.VMEM)
    extra = () if so_far is None else (so_far,)
    return pl.pallas_call(
        mix_body,
        out_shape=jax.ShapeDtypeStruct((toks, part * PARTS), dtype),
        in_specs=[here, pl.BlockSpec(memory_space=pl.ANY)] + [here for _ in extra],
        out_specs=pl.BlockSpec(memory_space=pl.ANY),
        scratch_shapes=[
            pltpu.VMEM((total, part), BF16),
            pltpu.VMEM((PARTS, total // PARTS, part), BF16),
            pltpu.VMEM((toks, part * PARTS), dtype),
            pltpu.SemaphoreType.DMA((total // BLOCK,)),
            pltpu.SemaphoreType.DMA((PARTS,)),
        ],
        compiler_params=pltpu.CompilerParams(vmem_limit_bytes=SMALL),
        cost_estimate=pl.CostEstimate(
            flops=2 * total * TILE * part, bytes_accessed=2 * total * part, transcendentals=0
        ),
        name="mix",
    )(weights, rows_in, *extra)


def exchange(rows, experts):
    part = rows.shape[1]
    rows = rows.reshape(experts, -1, part)
    return lax.all_to_all(rows, CHIPS, split_axis=0, concat_axis=0, tiled=True).reshape(-1, part)


def local(tokens, routes, gates, gate_weight, up_weight, down_weight):
    experts = lax.axis_size("group") * lax.axis_size("chip")
    swap = [(0, 1), (1, 0)]
    others = [lax.ppermute(w, "core", swap) for w in (gate_weight, up_weight, down_weight)]
    routes_t = routes.T
    firsts = [sum(SLOTS[:n]) for n in range(len(SLOTS))]
    packed = [pack(routes_t, tokens, n, f, experts) for n, f in zip(SLOTS, firsts)]
    arrived = [exchange(p, experts) for p in packed]
    done = [
        ffn(a, gate_weight, others[0], up_weight, others[1], down_weight, others[2])
        for a in arrived
    ]
    back = [exchange(d, experts) for d in done]
    mixed = None
    for at, weights in enumerate(plan(routes, gates, tuple(zip(SLOTS, firsts)), experts)):
        mixed = mix(weights, back[at], mixed, BF16 if at == len(SLOTS) - 1 else F32)
    return mixed


def solution(mesh):
    groups, members = mesh.devices.shape
    by_core = Mesh(mesh.devices.reshape(groups, members // 2, 2), AXES)
    placed = (
        P(AXES, None),
        P(AXES, None),
        P(AXES, None),
        P(AXES, None, None),
        P(AXES, None, None),
        P(AXES, None, None),
    )
    return jax.shard_map(
        local, mesh=by_core, in_specs=placed, out_specs=P(AXES, None), check_vma=False
    )
```
